32 devices in a mesh: aux: 8 (over z, core), pairs: 4 (over y, x).
Axes of the slice: x: 2, y: 2, z: 4, core: 2. Of those that a mesh axis runs over, the one named last changes fastest.
Arguments:
- amplitudes: bfloat16 [8, 256, 256], P(None, 'aux', 'pairs'), may hold values from -6 to 6
- three_index: bfloat16 [224, 256, 256], P('aux'), may hold values from -0.078125 to 0.078125
- virt_energy: float32 [256], replicated, may hold values from 0.2 to 1.5
- pair_energy: float32 [8], replicated, may hold values from -1.5 to -0.3
- owner: int32 [8], replicated, may hold values from 0 to 3, as said below
- partner: int32 [8], replicated, may hold values from 0 to 7, as said below
Outputs:
- blocks: float32 [16, 256, 256], P('pairs', 'aux')
The draws below stay inside these ranges and needn't reach their ends.
Inputs may be any that keep to these rules, and one draw needn't show every extreme that they name: `owner`: no group index is named by more than 4 pairs, and one group is named by exactly 4 pairs. partner[partner[p]] == p for every pair p.
All inputs are finite; a program needn't handle non-finite values.
Results may differ from the reference program's by a relative error of at most 0.0029.
Values may be sent and summed in bfloat16 or wider, within the bound.
A program may use at most 64 MiB of HBM per device.

```python
import jax
import jax.numpy as jnp
from jax import lax

V = 256
PAIR_DEV = 2
NAUX = 224
PAIRS = 8
CAP = 4
SLOTS = 16


def draw_owner(key, part):
    groups = PAIRS // PAIR_DEV
    key_busy, key_units, key_pairs = jax.random.split(jax.random.fold_in(key, 17), 3)
    busiest = jax.random.randint(key_busy, (), 0, groups)
    unit_ids = jnp.arange(PAIRS, dtype=jnp.int32)
    unit_group = unit_ids // PAIR_DEV
    unit_order = jax.random.permutation(key_units, PAIRS).astype(jnp.int32)
    guarded = (unit_ids == 0) | (unit_ids == PAIRS - 1)
    unit_score = unit_order + jnp.where(unit_group == busiest, PAIRS, 0) + jnp.where(guarded, 2 * PAIRS, 0)
    ranking = jnp.argsort(unit_score, stable=True)
    removed_units = ranking[:PAIR_DEV]
    group_ids = jnp.arange(groups, dtype=jnp.int32)
    removed = jnp.sum((unit_group[removed_units][:, None] == group_ids[None, :]).astype(jnp.int32), axis=0)
    counts = PAIR_DEV - removed + jnp.where(group_ids == busiest, PAIR_DEV, 0)
    cumulative = jnp.cumsum(counts)
    pair_rank = jax.random.permutation(key_pairs, PAIRS).astype(jnp.int32)
    return jnp.sum((cumulative[None, :] <= pair_rank[:, None]).astype(jnp.int32), axis=1).astype(jnp.int32)


def draw_partner(key, part):
    fixed_count = 2 * (PAIRS // 16)
    pair_order = jax.random.permutation(jax.random.fold_in(key, 29), PAIRS).astype(jnp.int32)
    rank_ids = jnp.arange(PAIRS, dtype=jnp.int32)
    mate_rank = jnp.where(rank_ids < fixed_count, rank_ids, fixed_count + (rank_ids - fixed_count ^ 1))
    return jnp.zeros((PAIRS,), jnp.int32).at[pair_order].set(pair_order[mate_rank]).astype(jnp.int32)


def steps_of(key, dims, pieces, smallest, largest):
    def one(dim, blocks):
        heights = jax.random.uniform(jax.random.fold_in(jax.random.fold_in(key, 6), dim), (blocks,), jnp.float32, smallest / len(pieces), largest / len(pieces))
        return jnp.repeat(jnp.exp(heights), dims[dim] // blocks).reshape((-1,) + (1,) * (len(dims) - dim - 1))

    gain = one(*pieces[0])
    for cut in pieces[1:]:
        gain = gain * one(*cut)
    return gain


def scatter_about(stream_key, dims, deviation, most, cuts=(), held_as=jnp.bfloat16):
    values = jax.random.normal(stream_key, dims, jnp.float32) * deviation
    if len(cuts) > 0:
        values = steps_of(stream_key, dims, cuts, -0.22, 0.18) * values
    return jnp.clip(values, min=-most, max=most).astype(held_as)


def setup_inputs(seed: int = 0) -> dict:
    key_of = jax.random.split(jax.random.key(seed), 7)
    amplitudes = scatter_about(key_of[0], (PAIRS, V, V), 1.0, 6.0, ((1, 8), (2, 4)))
    three_index = scatter_about(key_of[1], (NAUX, V, V), (V * 21) ** -0.5, 0.078125, ((0, 8),))
    virt_energy = jnp.clip(jax.random.uniform(key_of[2], (V,), jnp.float32, 0.2, 1.5), 0.2, 1.5)
    pair_energy = jnp.clip(jax.random.uniform(key_of[3], (PAIRS,), jnp.float32, -1.5, -0.3), -1.5, -0.3)
    owner = draw_owner(jax.random.fold_in(key_of[6], 71), 0)
    partner = draw_partner(jax.random.fold_in(key_of[6], 71), 0)
    return {"amplitudes": amplitudes, "three_index": three_index, "virt_energy": virt_energy, "pair_energy": pair_energy, "owner": owner, "partner": partner}


def reference(amplitudes, three_index, virt_energy, pair_energy, owner, partner):
    pair_ids = jnp.arange(PAIRS, dtype=jnp.int32)
    earlier = (owner[None, :] == owner[:, None]) & (pair_ids[None, :] < pair_ids[:, None])
    slot_rank = jnp.sum(earlier.astype(jnp.int32), axis=1).astype(jnp.int32)
    position = (owner * CAP + slot_rank).astype(jnp.int32)
    three_float = three_index.astype(jnp.float32)

    def ladder_one(amp_tile):
        half_product = jnp.einsum("cd,qbd->qcb", amp_tile.astype(jnp.float32), three_float)
        rounded = lax.optimization_barrier(half_product.astype(jnp.bfloat16))
        return jnp.einsum("qac,qcb->ab", three_float, rounded.astype(jnp.float32))

    ladder = lax.map(ladder_one, amplitudes)
    divisor = virt_energy[None, :, None] + virt_energy[None, None, :] - pair_energy[:, None, None]
    scaled = ladder / divisor
    combined = scaled + jnp.swapaxes(scaled[partner], 1, 2)
    blocks = jnp.zeros((SLOTS, V, V), jnp.float32).at[position].set(combined)
    return blocks
```

```python
import functools

import jax
import jax.numpy as jnp
from jax import lax
from jax.experimental import pallas as pl
from jax.experimental.pallas import tpu as pltpu
from jax.sharding import PartitionSpec as P

MESH = pl.DeviceIdType.MESH


def ladder_kernel(
    aux_size, groups,
    amp_ref, three_hbm, virt_ref, energy_ref, owner_ref, partner_ref,
    out_ref,
    three_buf, tiles, rows_all, sums, mate_in, z_out, z_in, gathered, virt_col,
    three_sem, tile_send, tile_recv, row_send, row_recv, fwd_send, fwd_recv,
    mate_send, mate_recv, z_send, z_recv, gat_send, gat_recv,
):
    pairs_all, rows, cols = amp_ref.shape
    naux, virt, _ = three_buf.shape
    per_group = pairs_all // groups
    chips = aux_size // 2
    capacity = out_ref.shape[0]
    me = lax.axis_index("aux")
    group = lax.axis_index("pairs")
    z, core = me // 2, lax.rem(me, 2)
    mate = z * 2 + (1 - core)

    def z_at(step):
        return lax.rem(z + step, chips)

    def group_at(step):
        return lax.rem(group + step, groups)

    load_three = pltpu.make_async_copy(three_hbm, three_buf, three_sem)
    load_three.start()

    barrier = pltpu.get_barrier_semaphore()
    pl.semaphore_signal(barrier, inc=1, device_id={"aux": mate, "pairs": group}, device_id_type=MESH)
    for k in range(1, chips):
        pl.semaphore_signal(
            barrier, inc=1, device_id={"aux": z_at(k) * 2 + core, "pairs": group}, device_id_type=MESH
        )
    for k in range(1, groups):
        pl.semaphore_signal(
            barrier, inc=1, device_id={"aux": me, "pairs": group_at(k)}, device_id_type=MESH
        )
    pl.semaphore_wait(barrier, 1 + (chips - 1) + (groups - 1))

    def to_mate(src, dst, send, recv):
        return pltpu.make_async_remote_copy(
            src_ref=src, dst_ref=dst, send_sem=send, recv_sem=recv,
            device_id={"aux": mate, "pairs": group}, device_id_type=MESH,
        )

    def to_chip(k, src, dst, send, recv):
        return pltpu.make_async_remote_copy(
            src_ref=src, dst_ref=dst, send_sem=send, recv_sem=recv,
            device_id={"aux": z_at(k) * 2 + core, "pairs": group}, device_id_type=MESH,
        )

    def to_group(k, src, dst, send, recv):
        return pltpu.make_async_remote_copy(
            src_ref=src, dst_ref=dst, send_sem=send, recv_sem=recv,
            device_id={"aux": me, "pairs": group_at(k)}, device_id_type=MESH,
        )

    tile_copies = [
        to_group(
            k, amp_ref.at[pl.ds(group_at(k) * per_group, per_group)], tiles.at[group],
            tile_send.at[k - 1], tile_recv.at[k - 1],
        )
        for k in range(1, groups)
    ]
    for copy in tile_copies:
        copy.start()
    tiles[group] = amp_ref[pl.ds(group * per_group, per_group)]
    virt_col[...] = jnp.transpose(jnp.broadcast_to(virt_ref[...], (128, virt)))
    for copy in tile_copies:
        copy.wait_recv()
    rows_all[me] = jnp.concatenate([tiles[j] for j in range(groups)], axis=-1)

    row_copies = [
        to_chip(k, rows_all.at[me], rows_all.at[me], row_send.at[k - 1], row_recv.at[k - 1])
        for k in range(1, chips)
    ]
    for copy in row_copies:
        copy.start()
    fwd_copies = []
    for k in range(chips):
        if k > 0:
            row_copies[k - 1].wait_recv()
        held = rows_all.at[z_at(chips - k) * 2 + core]
        copy = to_mate(held, held, fwd_send.at[k], fwd_recv.at[k])
        copy.start()
        fwd_copies.append(copy)
    load_three.wait()
    for copy in fwd_copies:
        copy.wait_recv()

    unroll = max(u for u in (1, 2, 3, 4) if naux % u == 0)
    trips = naux // unroll

    def ladder(p, first, last):
        def one(i, carry):
            amp = rows_all[:, p].reshape(virt, virt)
            lefts, halves = [], []
            for j in range(unroll):
                left = three_buf[i * unroll + j]
                half = lax.dot_general(
                    amp, left, (((1,), (1,)), ((), ())), preferred_element_type=jnp.float32
                )
                lefts.append(left)
                halves.append(half.astype(jnp.bfloat16))
            term = jnp.dot(
                jnp.concatenate(lefts, axis=1), jnp.concatenate(halves, axis=0),
                preferred_element_type=jnp.float32,
            )
            sums[p, 0] = sums[p, 0] + term.reshape(chips, 2, rows, virt)
            return carry

        lax.fori_loop(first, last, one, 0)

    def send_mate(p):
        whole = sums[p, 0].reshape(virt, virt)
        sums[p, 1] = jnp.transpose(whole).reshape(chips, 2, rows, virt)
        copy = to_mate(sums.at[p, :, :, 1 - core], mate_in.at[p], mate_send.at[p], mate_recv.at[p])
        copy.start()
        return copy

    def send_z(p, mate_copy):
        mate_copy.wait_recv()
        copies = []
        for k in range(1, chips):
            there = z_at(k)
            both = sums[p, :, there, core] + mate_in[p, :, there]
            z_out[p, k - 1] = both.astype(jnp.bfloat16)
            copy = to_chip(k, z_out.at[p, k - 1], z_in.at[p, k - 1], z_send.at[p, k - 1], z_recv.at[p, k - 1])
            copy.start()
            copies.append(copy)
        return copies

    def finish(p, z_copies):
        total = sums[p, :, z, core] + mate_in[p, :, z]
        for k, copy in enumerate(z_copies):
            copy.wait_recv()
            total = total + z_in[p, k].astype(jnp.float32)
        here = virt_col[pl.ds(me * rows, rows), 0:1]
        divisor = here + virt_ref[...] - energy_ref[group * per_group + p]
        mine = group * per_group + p
        gathered[mine] = (total / divisor[None]).astype(jnp.bfloat16)
        copies = []
        for k in range(1, groups):
            copy = to_group(
                k, gathered.at[mine], gathered.at[mine], gat_send.at[p, k - 1], gat_recv.at[p, k - 1]
            )
            copy.start()
            copies.append(copy)
        return copies

    sums[:, 0] = jnp.zeros((per_group, chips, 2, rows, virt), jnp.float32)
    mate_copies, z_copies, gat_copies = [], [], []
    for p in range(per_group):
        ladder(p, 0, trips // 2)
        if p > 0:
            z_copies.append(send_z(p - 1, mate_copies[p - 1]))
        ladder(p, trips // 2, trips)
        mate_copies.append(send_mate(p))
        if p > 0:
            gat_copies.append(finish(p - 1, z_copies[p - 1]))
    z_copies.append(send_z(per_group - 1, mate_copies[-1]))
    gat_copies.append(finish(per_group - 1, z_copies[-1]))

    count = jnp.int32(0)
    sources = [jnp.int32(0) for _ in range(capacity)]
    for p in range(pairs_all):
        held = owner_ref[p] == group
        sources = [
            jnp.where(jnp.logical_and(held, count == s), jnp.int32(p), src) for s, src in enumerate(sources)
        ]
        count = count + jnp.where(held, jnp.int32(1), jnp.int32(0))

    for copies in gat_copies:
        for copy in copies:
            copy.wait_recv()
    for s in range(capacity):
        other = partner_ref[sources[s]]
        block = gathered[sources[s]][0].astype(jnp.float32) + gathered[other][1].astype(jnp.float32)
        out_ref[s] = jnp.where(count > s, block, 0.0)

    for copy in tile_copies + row_copies + fwd_copies + mate_copies:
        copy.wait_send()
    for copies in z_copies + gat_copies:
        for copy in copies:
            copy.wait_send()


def per_device(aux_size, groups, amplitudes, three_index, virt_energy, pair_energy, owner, partner):
    pairs_all, rows, cols = amplitudes.shape
    naux, virt, _ = three_index.shape
    per_group = pairs_all // groups
    capacity = 2 * per_group
    chips = aux_size // 2
    dma = pltpu.SemaphoreType.DMA
    vmem = pl.BlockSpec(memory_space=pltpu.VMEM)
    smem = pl.BlockSpec(memory_space=pltpu.SMEM)
    return pl.pallas_call(
        functools.partial(ladder_kernel, aux_size, groups),
        out_shape=jax.ShapeDtypeStruct((capacity, rows, virt), jnp.float32),
        in_specs=[vmem, pl.BlockSpec(memory_space=pl.ANY), vmem, smem, smem, smem],
        out_specs=vmem,
        scratch_shapes=[
            pltpu.VMEM((naux, virt, virt), jnp.bfloat16),
            pltpu.VMEM((groups, per_group, rows, cols), jnp.bfloat16),
            pltpu.VMEM((aux_size, per_group, rows, virt), jnp.bfloat16),
            pltpu.VMEM((per_group, 2, chips, 2, rows, virt), jnp.float32),
            pltpu.VMEM((per_group, 2, chips, rows, virt), jnp.float32),
            pltpu.VMEM((per_group, chips - 1, 2, rows, virt), jnp.bfloat16),
            pltpu.VMEM((per_group, chips - 1, 2, rows, virt), jnp.bfloat16),
            pltpu.VMEM((pairs_all, 2, rows, virt), jnp.bfloat16),
            pltpu.VMEM((virt, 128), jnp.float32),
            dma,
            dma((groups - 1,)), dma((groups - 1,)),
            dma((chips - 1,)), dma((chips - 1,)),
            dma((chips,)), dma((chips,)),
            dma((per_group,)), dma((per_group,)),
            dma((per_group, chips - 1)), dma((per_group, chips - 1)),
            dma((per_group, groups - 1)), dma((per_group, groups - 1)),
        ],
        compiler_params=pltpu.CompilerParams(
            collective_id=0, has_side_effects=True, vmem_limit_bytes=40 * 1024 * 1024
        ),
        cost_estimate=pl.CostEstimate(
            flops=4 * per_group * naux * virt**3, bytes_accessed=2 * naux * virt**2, transcendentals=0
        ),
    )(amplitudes, three_index, virt_energy.reshape(1, virt), pair_energy, owner, partner)


def solution(mesh):
    placed = (P(None, "aux", "pairs"), P("aux", None, None), P(), P(), P(), P())
    return jax.shard_map(
        functools.partial(per_device, mesh.shape["aux"], mesh.shape["pairs"]),
        mesh=mesh, in_specs=placed, out_specs=P("pairs", "aux", None), check_vma=False,
    )
```

```python
import functools

import jax
import jax.numpy as jnp
from jax import lax
from jax.experimental import pallas as pl
from jax.experimental.pallas import tpu as pltpu
from jax.sharding import PartitionSpec as P

MESH = pl.DeviceIdType.MESH


def ladder_kernel(
    aux_size, groups,
    amp_ref, three_hbm, virt_hbm, energy_hbm, owner_hbm, partner_hbm,
    out_ref,
    virt_ref, energy_ref, owner_ref, partner_ref, small_sem, own_sem, three_buf, tiles, rows_all, sums, mate_in, z_out, z_in, gathered, virt_col,
    three_sem, tile_send, tile_recv, row_send, row_recv, fwd_send, fwd_recv,
    mate_send, mate_recv, z_send, z_recv, gat_send, gat_recv,
):
    pairs_all, rows, cols = amp_ref.shape
    naux, virt, _ = three_buf.shape
    per_group = pairs_all // groups
    chips = aux_size // 2
    capacity = out_ref.shape[0]
    me = lax.axis_index("aux")
    group = lax.axis_index("pairs")
    z, core = me // 2, lax.rem(me, 2)
    mate = z * 2 + (1 - core)

    def z_at(step):
        return lax.rem(z + step, chips)

    def group_at(step):
        return lax.rem(group + step, groups)

    load_three = pltpu.make_async_copy(three_hbm, three_buf, three_sem)
    load_three.start()
    own_tile = pltpu.make_async_copy(
        amp_ref.at[pl.ds(group * per_group, per_group)], tiles.at[group], own_sem
    )
    own_tile.start()
    small_loads = [
        pltpu.make_async_copy(src, dst, small_sem.at[i])
        for i, (src, dst) in enumerate(
            [(virt_hbm, virt_ref), (energy_hbm, energy_ref), (owner_hbm, owner_ref), (partner_hbm, partner_ref)]
        )
    ]
    for load in small_loads:
        load.start()

    barrier = pltpu.get_barrier_semaphore()
    pl.semaphore_signal(barrier, inc=1, device_id={"aux": mate, "pairs": group}, device_id_type=MESH)
    for k in range(1, chips):
        pl.semaphore_signal(
            barrier, inc=1, device_id={"aux": z_at(k) * 2 + core, "pairs": group}, device_id_type=MESH
        )
    for k in range(1, groups):
        pl.semaphore_signal(
            barrier, inc=1, device_id={"aux": me, "pairs": group_at(k)}, device_id_type=MESH
        )
    pl.semaphore_wait(barrier, 1 + (chips - 1) + (groups - 1))

    def to_mate(src, dst, send, recv):
        return pltpu.make_async_remote_copy(
            src_ref=src, dst_ref=dst, send_sem=send, recv_sem=recv,
            device_id={"aux": mate, "pairs": group}, device_id_type=MESH,
        )

    def to_chip(k, src, dst, send, recv):
        return pltpu.make_async_remote_copy(
            src_ref=src, dst_ref=dst, send_sem=send, recv_sem=recv,
            device_id={"aux": z_at(k) * 2 + core, "pairs": group}, device_id_type=MESH,
        )

    def to_group(k, src, dst, send, recv):
        return pltpu.make_async_remote_copy(
            src_ref=src, dst_ref=dst, send_sem=send, recv_sem=recv,
            device_id={"aux": me, "pairs": group_at(k)}, device_id_type=MESH,
        )

    tile_copies = [
        to_group(
            k, amp_ref.at[pl.ds(group_at(k) * per_group, per_group)], tiles.at[group],
            tile_send.at[k - 1], tile_recv.at[k - 1],
        )
        for k in range(1, groups)
    ]
    for copy in tile_copies:
        copy.start()
    for load in small_loads:
        load.wait()
    virt_col[...] = jnp.transpose(jnp.broadcast_to(virt_ref[...], (128, virt)))
    own_tile.wait()
    for copy in tile_copies:
        copy.wait_recv()
    rows_all[me] = jnp.concatenate([tiles[j] for j in range(groups)], axis=-1)

    row_copies = [
        to_chip(k, rows_all.at[me], rows_all.at[me], row_send.at[k - 1], row_recv.at[k - 1])
        for k in range(1, chips)
    ]
    for copy in row_copies:
        copy.start()
    fwd_copies = []
    for k in range(chips):
        if k > 0:
            row_copies[k - 1].wait_recv()
        held = rows_all.at[z_at(chips - k) * 2 + core]
        copy = to_mate(held, held, fwd_send.at[k], fwd_recv.at[k])
        copy.start()
        fwd_copies.append(copy)
    load_three.wait()
    for copy in fwd_copies:
        copy.wait_recv()

    unroll = max(u for u in (1, 2, 3, 4) if naux % u == 0)
    trips = naux // unroll

    def ladder(p, first, last):
        def one(i, carry):
            amp = rows_all[:, p].reshape(virt, virt)
            lefts, halves = [], []
            for j in range(unroll):
                left = three_buf[i * unroll + j]
                half = lax.dot_general(
                    amp, left, (((1,), (1,)), ((), ())), preferred_element_type=jnp.float32
                )
                lefts.append(left)
                halves.append(half.astype(jnp.bfloat16))
            term = jnp.dot(
                jnp.concatenate(lefts, axis=1), jnp.concatenate(halves, axis=0),
                preferred_element_type=jnp.float32,
            )
            sums[p, 0] = sums[p, 0] + term.reshape(chips, 2, rows, virt)
            return carry

        lax.fori_loop(first, last, one, 0)

    def send_mate(p):
        whole = sums[p, 0].reshape(virt, virt)
        sums[p, 1] = jnp.transpose(whole).reshape(chips, 2, rows, virt)
        copy = to_mate(sums.at[p, :, :, 1 - core], mate_in.at[p], mate_send.at[p], mate_recv.at[p])
        copy.start()
        return copy

    def send_z(p, mate_copy):
        mate_copy.wait_recv()
        copies = []
        for k in range(1, chips):
            there = z_at(k)
            both = sums[p, :, there, core] + mate_in[p, :, there]
            z_out[p, k - 1] = both.astype(jnp.bfloat16)
            copy = to_chip(k, z_out.at[p, k - 1], z_in.at[p, k - 1], z_send.at[p, k - 1], z_recv.at[p, k - 1])
            copy.start()
            copies.append(copy)
        return copies

    def finish(p, z_copies):
        total = sums[p, :, z, core] + mate_in[p, :, z]
        for k, copy in enumerate(z_copies):
            copy.wait_recv()
            total = total + z_in[p, k].astype(jnp.float32)
        here = virt_col[pl.ds(me * rows, rows), 0:1]
        divisor = here + virt_ref[...] - energy_ref[group * per_group + p]
        mine = group * per_group + p
        gathered[mine] = (total / divisor[None]).astype(jnp.bfloat16)
        copies = []
        for k in range(1, groups):
            copy = to_group(
                k, gathered.at[mine], gathered.at[mine], gat_send.at[p, k - 1], gat_recv.at[p, k - 1]
            )
            copy.start()
            copies.append(copy)
        return copies

    sums[:, 0] = jnp.zeros((per_group, chips, 2, rows, virt), jnp.float32)
    mate_copies, z_copies, gat_copies = [], [], []
    for p in range(per_group):
        ladder(p, 0, trips // 2)
        if p > 0:
            z_copies.append(send_z(p - 1, mate_copies[p - 1]))
        ladder(p, trips // 2, trips)
        mate_copies.append(send_mate(p))
        if p > 0:
            gat_copies.append(finish(p - 1, z_copies[p - 1]))
    z_copies.append(send_z(per_group - 1, mate_copies[-1]))
    gat_copies.append(finish(per_group - 1, z_copies[-1]))

    count = jnp.int32(0)
    sources = [jnp.int32(0) for _ in range(capacity)]
    for p in range(pairs_all):
        held = owner_ref[p] == group
        sources = [
            jnp.where(jnp.logical_and(held, count == s), jnp.int32(p), src) for s, src in enumerate(sources)
        ]
        count = count + jnp.where(held, jnp.int32(1), jnp.int32(0))

    for copies in gat_copies:
        for copy in copies:
            copy.wait_recv()
    for s in range(capacity):
        other = partner_ref[sources[s]]
        block = gathered[sources[s]][0].astype(jnp.float32) + gathered[other][1].astype(jnp.float32)
        out_ref[s] = jnp.where(count > s, block, 0.0)

    for copy in tile_copies + row_copies + fwd_copies + mate_copies:
        copy.wait_send()
    for copies in z_copies + gat_copies:
        for copy in copies:
            copy.wait_send()


def per_device(aux_size, groups, amplitudes, three_index, virt_energy, pair_energy, owner, partner):
    pairs_all, rows, cols = amplitudes.shape
    naux, virt, _ = three_index.shape
    per_group = pairs_all // groups
    capacity = 2 * per_group
    chips = aux_size // 2
    dma = pltpu.SemaphoreType.DMA
    vmem = pl.BlockSpec(memory_space=pltpu.VMEM)
    hbm = pl.BlockSpec(memory_space=pltpu.HBM)
    return pl.pallas_call(
        functools.partial(ladder_kernel, aux_size, groups),
        out_shape=jax.ShapeDtypeStruct((capacity, rows, virt), jnp.float32),
        in_specs=[hbm] * 6,
        out_specs=vmem,
        scratch_shapes=[
            pltpu.VMEM((1, virt), jnp.float32),
            pltpu.SMEM((pairs_all,), jnp.float32),
            pltpu.SMEM((pairs_all,), jnp.int32),
            pltpu.SMEM((pairs_all,), jnp.int32),
            dma((4,)),
            dma,
            pltpu.VMEM((naux, virt, virt), jnp.bfloat16),
            pltpu.VMEM((groups, per_group, rows, cols), jnp.bfloat16),
            pltpu.VMEM((aux_size, per_group, rows, virt), jnp.bfloat16),
            pltpu.VMEM((per_group, 2, chips, 2, rows, virt), jnp.float32),
            pltpu.VMEM((per_group, 2, chips, rows, virt), jnp.float32),
            pltpu.VMEM((per_group, chips - 1, 2, rows, virt), jnp.bfloat16),
            pltpu.VMEM((per_group, chips - 1, 2, rows, virt), jnp.bfloat16),
            pltpu.VMEM((pairs_all, 2, rows, virt), jnp.bfloat16),
            pltpu.VMEM((virt, 128), jnp.float32),
            dma,
            dma((groups - 1,)), dma((groups - 1,)),
            dma((chips - 1,)), dma((chips - 1,)),
            dma((chips,)), dma((chips,)),
            dma((per_group,)), dma((per_group,)),
            dma((per_group, chips - 1)), dma((per_group, chips - 1)),
            dma((per_group, groups - 1)), dma((per_group, groups - 1)),
        ],
        compiler_params=pltpu.CompilerParams(
            collective_id=0, has_side_effects=True, vmem_limit_bytes=60 * 1024 * 1024
        ),
        cost_estimate=pl.CostEstimate(
            flops=4 * per_group * naux * virt**3, bytes_accessed=2 * naux * virt**2, transcendentals=0
        ),
    )(amplitudes, three_index, virt_energy.reshape(1, virt), pair_energy, owner, partner)


def solution(mesh):
    placed = (P(None, "aux", "pairs"), P("aux", None, None), P(), P(), P(), P())
    return jax.shard_map(
        functools.partial(per_device, mesh.shape["aux"], mesh.shape["pairs"]),
        mesh=mesh, in_specs=placed, out_specs=P("pairs", "aux", None), check_vma=False,
    )
```

```python
import functools

import jax
import jax.numpy as jnp
from jax import lax
from jax.experimental import pallas as pl
from jax.experimental.pallas import tpu as pltpu
from jax.sharding import PartitionSpec as P

MESH = pl.DeviceIdType.MESH


def ladder_kernel(
    aux_size, groups,
    amp_ref, three_hbm, virt_hbm, energy_hbm, owner_hbm, partner_hbm,
    out_ref,
    virt_ref, energy_ref, owner_ref, partner_ref, small_sem, own_sem, amp_buf, packed, three_buf, tiles, rows_all, sums, mate_in, z_out, z_in, gathered, virt_col,
    three_sem, tile_send, tile_recv, row_send, row_recv, fwd_send, fwd_recv,
    mate_send, mate_recv, z_send, z_recv, gat_send, gat_recv,
):
    pairs_all, rows, cols = amp_ref.shape
    naux, virt, _ = three_buf.shape
    per_group = pairs_all // groups
    chips = aux_size // 2
    capacity = out_ref.shape[0]
    me = lax.axis_index("aux")
    group = lax.axis_index("pairs")
    z, core = me // 2, lax.rem(me, 2)
    mate = z * 2 + (1 - core)

    def z_at(step):
        return lax.rem(z + step, chips)

    def group_at(step):
        return lax.rem(group + step, groups)

    load_amp = pltpu.make_async_copy(amp_ref, amp_buf, own_sem)
    load_amp.start()
    load_three = pltpu.make_async_copy(three_hbm, three_buf, three_sem)
    load_three.start()
    small_loads = [
        pltpu.make_async_copy(src, dst, small_sem.at[i])
        for i, (src, dst) in enumerate(
            [(virt_hbm, virt_ref), (energy_hbm, energy_ref), (owner_hbm, owner_ref), (partner_hbm, partner_ref)]
        )
    ]
    for load in small_loads:
        load.start()

    barrier = pltpu.get_barrier_semaphore()
    pl.semaphore_signal(barrier, inc=1, device_id={"aux": mate, "pairs": group}, device_id_type=MESH)
    for k in range(1, chips):
        pl.semaphore_signal(
            barrier, inc=1, device_id={"aux": z_at(k) * 2 + core, "pairs": group}, device_id_type=MESH
        )
    for k in range(1, groups):
        pl.semaphore_signal(
            barrier, inc=1, device_id={"aux": me, "pairs": group_at(k)}, device_id_type=MESH
        )
    load_amp.wait()
    for j in range(groups):
        packed[j] = jnp.concatenate([amp_buf[j * per_group + q] for q in range(per_group)], axis=-1)
    tiles[group] = packed[group]
    pl.semaphore_wait(barrier, 1 + (chips - 1) + (groups - 1))

    def to_mate(src, dst, send, recv):
        return pltpu.make_async_remote_copy(
            src_ref=src, dst_ref=dst, send_sem=send, recv_sem=recv,
            device_id={"aux": mate, "pairs": group}, device_id_type=MESH,
        )

    def to_chip(k, src, dst, send, recv):
        return pltpu.make_async_remote_copy(
            src_ref=src, dst_ref=dst, send_sem=send, recv_sem=recv,
            device_id={"aux": z_at(k) * 2 + core, "pairs": group}, device_id_type=MESH,
        )

    def to_group(k, src, dst, send, recv):
        return pltpu.make_async_remote_copy(
            src_ref=src, dst_ref=dst, send_sem=send, recv_sem=recv,
            device_id={"aux": me, "pairs": group_at(k)}, device_id_type=MESH,
        )

    tile_copies = [
        to_group(
            k, packed.at[group_at(k)], tiles.at[group],
            tile_send.at[k - 1], tile_recv.at[k - 1],
        )
        for k in range(1, groups)
    ]
    for copy in tile_copies:
        copy.start()
    for load in small_loads:
        load.wait()
    virt_col[...] = jnp.transpose(jnp.broadcast_to(virt_ref[...], (128, virt)))
    for copy in tile_copies:
        copy.wait_recv()
    for q in range(per_group):
        rows_all[me, q] = jnp.concatenate(
            [tiles[j][:, q * cols : (q + 1) * cols] for j in range(groups)], axis=-1
        )

    row_copies = [
        to_chip(k, rows_all.at[me], rows_all.at[me], row_send.at[k - 1], row_recv.at[k - 1])
        for k in range(1, chips)
    ]
    for copy in row_copies:
        copy.start()
    fwd_copies = []
    for k in range(chips):
        if k > 0:
            row_copies[k - 1].wait_recv()
        held = rows_all.at[z_at(chips - k) * 2 + core]
        copy = to_mate(held, held, fwd_send.at[k], fwd_recv.at[k])
        copy.start()
        fwd_copies.append(copy)
    load_three.wait()
    for copy in fwd_copies:
        copy.wait_recv()

    unroll = max(u for u in range(1, 15) if naux % u == 0)
    trips = naux // unroll

    def ladder(p, first, last):
        def one(i, carry):
            amp = rows_all[:, p].reshape(virt, virt)
            lefts, halves = [], []
            for j in range(unroll):
                left = three_buf[i * unroll + j]
                half = lax.dot_general(
                    amp, left, (((1,), (1,)), ((), ())), preferred_element_type=jnp.float32
                )
                lefts.append(left)
                halves.append(half.astype(jnp.bfloat16))
            term = jnp.dot(
                jnp.concatenate(lefts, axis=1), jnp.concatenate(halves, axis=0),
                preferred_element_type=jnp.float32,
            )
            sums[p, 0] = sums[p, 0] + term.reshape(chips, 2, rows, virt)
            return carry

        lax.fori_loop(first, last, one, 0)

    def send_mate(p):
        whole = sums[p, 0].reshape(virt, virt)
        sums[p, 1] = jnp.transpose(whole).reshape(chips, 2, rows, virt)
        copy = to_mate(sums.at[p, :, :, 1 - core], mate_in.at[p], mate_send.at[p], mate_recv.at[p])
        copy.start()
        return copy

    def send_z(p, mate_copy):
        mate_copy.wait_recv()
        copies = []
        for k in range(1, chips):
            there = z_at(k)
            both = sums[p, :, there, core] + mate_in[p, :, there]
            z_out[p, k - 1] = both.astype(jnp.bfloat16)
            copy = to_chip(k, z_out.at[p, k - 1], z_in.at[p, k - 1], z_send.at[p, k - 1], z_recv.at[p, k - 1])
            copy.start()
            copies.append(copy)
        return copies

    def finish(p, z_copies):
        total = sums[p, :, z, core] + mate_in[p, :, z]
        for k, copy in enumerate(z_copies):
            copy.wait_recv()
            total = total + z_in[p, k].astype(jnp.float32)
        here = virt_col[pl.ds(me * rows, rows), 0:1]
        divisor = here + virt_ref[...] - energy_ref[group * per_group + p]
        mine = group * per_group + p
        gathered[mine] = (total / divisor[None]).astype(jnp.bfloat16)
        copies = []
        for k in range(1, groups):
            copy = to_group(
                k, gathered.at[mine], gathered.at[mine], gat_send.at[p, k - 1], gat_recv.at[p, k - 1]
            )
            copy.start()
            copies.append(copy)
        return copies

    sums[:, 0] = jnp.zeros((per_group, chips, 2, rows, virt), jnp.float32)
    mate_copies, z_copies, gat_copies = [], [], []
    for p in range(per_group):
        ladder(p, 0, trips // 2)
        if p > 0:
            z_copies.append(send_z(p - 1, mate_copies[p - 1]))
        ladder(p, trips // 2, trips)
        mate_copies.append(send_mate(p))
        if p > 0:
            gat_copies.append(finish(p - 1, z_copies[p - 1]))
    z_copies.append(send_z(per_group - 1, mate_copies[-1]))
    gat_copies.append(finish(per_group - 1, z_copies[-1]))

    count = jnp.int32(0)
    sources = [jnp.int32(0) for _ in range(capacity)]
    for p in range(pairs_all):
        held = owner_ref[p] == group
        sources = [
            jnp.where(jnp.logical_and(held, count == s), jnp.int32(p), src) for s, src in enumerate(sources)
        ]
        count = count + jnp.where(held, jnp.int32(1), jnp.int32(0))

    for copies in gat_copies:
        for copy in copies:
            copy.wait_recv()
    for s in range(capacity):
        other = partner_ref[sources[s]]
        block = gathered[sources[s]][0].astype(jnp.float32) + gathered[other][1].astype(jnp.float32)
        out_ref[s] = jnp.where(count > s, block, 0.0)

    for copy in tile_copies + row_copies + fwd_copies + mate_copies:
        copy.wait_send()
    for copies in z_copies + gat_copies:
        for copy in copies:
            copy.wait_send()


def per_device(aux_size, groups, amplitudes, three_index, virt_energy, pair_energy, owner, partner):
    pairs_all, rows, cols = amplitudes.shape
    naux, virt, _ = three_index.shape
    per_group = pairs_all // groups
    capacity = 2 * per_group
    chips = aux_size // 2
    dma = pltpu.SemaphoreType.DMA
    vmem = pl.BlockSpec(memory_space=pltpu.VMEM)
    hbm = pl.BlockSpec(memory_space=pltpu.HBM)
    return pl.pallas_call(
        functools.partial(ladder_kernel, aux_size, groups),
        out_shape=pltpu.VMEM((capacity, rows, virt), jnp.float32),
        in_specs=[hbm] * 6,
        out_specs=vmem,
        scratch_shapes=[
            pltpu.VMEM((1, virt), jnp.float32),
            pltpu.SMEM((pairs_all,), jnp.float32),
            pltpu.SMEM((pairs_all,), jnp.int32),
            pltpu.SMEM((pairs_all,), jnp.int32),
            dma((4,)),
            dma,
            pltpu.VMEM(amplitudes.shape, jnp.bfloat16),
            pltpu.VMEM((groups, rows, per_group * cols), jnp.bfloat16),
            pltpu.VMEM((naux, virt, virt), jnp.bfloat16),
            pltpu.VMEM((groups, rows, per_group * cols), jnp.bfloat16),
            pltpu.VMEM((aux_size, per_group, rows, virt), jnp.bfloat16),
            pltpu.VMEM((per_group, 2, chips, 2, rows, virt), jnp.float32),
            pltpu.VMEM((per_group, 2, chips, rows, virt), jnp.float32),
            pltpu.VMEM((per_group, chips - 1, 2, rows, virt), jnp.bfloat16),
            pltpu.VMEM((per_group, chips - 1, 2, rows, virt), jnp.bfloat16),
            pltpu.VMEM((pairs_all, 2, rows, virt), jnp.bfloat16),
            pltpu.VMEM((virt, 128), jnp.float32),
            dma,
            dma((groups - 1,)), dma((groups - 1,)),
            dma((chips - 1,)), dma((chips - 1,)),
            dma((chips,)), dma((chips,)),
            dma((per_group,)), dma((per_group,)),
            dma((per_group, chips - 1)), dma((per_group, chips - 1)),
            dma((per_group, groups - 1)), dma((per_group, groups - 1)),
        ],
        compiler_params=pltpu.CompilerParams(
            collective_id=0, has_side_effects=True, vmem_limit_bytes=60 * 1024 * 1024
        ),
        cost_estimate=pl.CostEstimate(
            flops=4 * per_group * naux * virt**3, bytes_accessed=2 * naux * virt**2, transcendentals=0
        ),
    )(amplitudes, three_index, virt_energy.reshape(1, virt), pair_energy, owner, partner)


def solution(mesh):
    placed = (P(None, "aux", "pairs"), P("aux", None, None), P(), P(), P(), P())
    return jax.shard_map(
        functools.partial(per_device, mesh.shape["aux"], mesh.shape["pairs"]),
        mesh=mesh, in_specs=placed, out_specs=P("pairs", "aux", None), check_vma=False,
    )
```

```python
import functools

import jax
import jax.numpy as jnp
from jax import lax
from jax.experimental import pallas as pl
from jax.experimental.pallas import tpu as pltpu
from jax.sharding import PartitionSpec as P

MESH = pl.DeviceIdType.MESH


def ladder_kernel(
    aux_size, groups,
    amp_ref, three_hbm, virt_hbm, energy_hbm, owner_hbm, partner_hbm,
    out_ref,
    virt_ref, energy_ref, owner_ref, partner_ref, small_sem, own_sem, amp_buf, packed, three_buf, tiles, rows_all, sums, mate_in, z_out, z_in, gathered, virt_col,
    three_sem, tile_send, tile_recv, fwd_send, fwd_recv,
    mate_send, mate_recv, z_send, z_recv, gat_send, gat_recv,
):
    pairs_all, rows, cols = amp_ref.shape
    naux, virt, _ = three_buf.shape
    per_group = pairs_all // groups
    chips = aux_size // 2
    capacity = out_ref.shape[0]
    me = lax.axis_index("aux")
    group = lax.axis_index("pairs")
    z, core = me // 2, lax.rem(me, 2)
    mate = z * 2 + (1 - core)

    def z_at(step):
        return lax.rem(z + step, chips)

    def group_at(step):
        return lax.rem(group + step, groups)

    load_amp = pltpu.make_async_copy(amp_ref, amp_buf, own_sem)
    load_amp.start()
    load_three = pltpu.make_async_copy(three_hbm, three_buf, three_sem)
    load_three.start()
    small_loads = [
        pltpu.make_async_copy(src, dst, small_sem.at[i])
        for i, (src, dst) in enumerate(
            [(virt_hbm, virt_ref), (energy_hbm, energy_ref), (owner_hbm, owner_ref), (partner_hbm, partner_ref)]
        )
    ]
    for load in small_loads:
        load.start()

    barrier = pltpu.get_barrier_semaphore()
    pl.semaphore_signal(barrier, inc=1, device_id={"aux": mate, "pairs": group}, device_id_type=MESH)
    others = [(k, m) for k in range(chips) for m in range(groups) if k or m]
    for k, m in others:
        pl.semaphore_signal(
            barrier, inc=1, device_id={"aux": z_at(k) * 2 + core, "pairs": group_at(m)}, device_id_type=MESH
        )

    load_amp.wait()
    for j in range(groups):
        packed[j] = jnp.concatenate([amp_buf[j * per_group + q] for q in range(per_group)], axis=-1)
    tiles[me, group] = packed[group]
    pl.semaphore_wait(barrier, 1 + len(others))

    def to_mate(src, dst, send, recv):
        return pltpu.make_async_remote_copy(
            src_ref=src, dst_ref=dst, send_sem=send, recv_sem=recv,
            device_id={"aux": mate, "pairs": group}, device_id_type=MESH,
        )

    def to_chip(k, src, dst, send, recv):
        return pltpu.make_async_remote_copy(
            src_ref=src, dst_ref=dst, send_sem=send, recv_sem=recv,
            device_id={"aux": z_at(k) * 2 + core, "pairs": group}, device_id_type=MESH,
        )

    def to_group(k, src, dst, send, recv):
        return pltpu.make_async_remote_copy(
            src_ref=src, dst_ref=dst, send_sem=send, recv_sem=recv,
            device_id={"aux": me, "pairs": group_at(k)}, device_id_type=MESH,
        )

    tile_copies = {
        (k, m): pltpu.make_async_remote_copy(
            src_ref=packed.at[group_at(m)], dst_ref=tiles.at[me, group],
            send_sem=tile_send.at[k, m], recv_sem=tile_recv.at[k, m],
            device_id={"aux": z_at(k) * 2 + core, "pairs": group_at(m)}, device_id_type=MESH,
        )
        for k, m in others
    }
    for copy in tile_copies.values():
        copy.start()
    for load in small_loads:
        load.wait()
    virt_col[...] = jnp.transpose(jnp.broadcast_to(virt_ref[...], (128, virt)))

    fwd_copies = []
    for k in range(chips):
        for m in range(groups):
            if k or m:
                tile_copies[k, m].wait_recv()
        held = tiles.at[z_at(chips - k) * 2 + core]
        copy = to_mate(held, held, fwd_send.at[k], fwd_recv.at[k])
        copy.start()
        fwd_copies.append(copy)
    load_three.wait()
    for copy in fwd_copies:
        copy.wait_recv()
    for a in range(aux_size):
        for q in range(per_group):
            rows_all[a, q] = jnp.concatenate(
                [tiles[a, j][:, q * cols : (q + 1) * cols] for j in range(groups)], axis=-1
            )

    unroll = max(u for u in range(1, 15) if naux % u == 0)
    trips = naux // unroll

    def ladder(p, first, last):
        def one(i, carry, fresh=False):
            amp = rows_all[:, p].reshape(virt, virt)
            lefts, halves = [], []
            for j in range(unroll):
                left = three_buf[i * unroll + j]
                half = lax.dot_general(
                    amp, left, (((1,), (1,)), ((), ())), preferred_element_type=jnp.float32
                )
                lefts.append(left)
                halves.append(half.astype(jnp.bfloat16))
            term = jnp.dot(
                jnp.concatenate(lefts, axis=1), jnp.concatenate(halves, axis=0),
                preferred_element_type=jnp.float32,
            )
            term = term.reshape(chips, 2, rows, virt)
            sums[p, 0] = term if fresh else sums[p, 0] + term
            return carry

        if first == 0 and last > 0:
            first = 1
            one(0, 0, fresh=True)
        lax.fori_loop(first, last, one, 0)

    def send_mate(p):
        whole = sums[p, 0].reshape(virt, virt)
        sums[p, 1] = jnp.transpose(whole).reshape(chips, 2, rows, virt)
        copy = to_mate(sums.at[p, :, :, 1 - core], mate_in.at[p], mate_send.at[p], mate_recv.at[p])
        copy.start()
        return copy

    def send_z(p, mate_copy):
        mate_copy.wait_recv()
        copies = []
        for k in range(1, chips):
            there = z_at(k)
            both = sums[p, :, there, core] + mate_in[p, :, there]
            z_out[p, k - 1] = both.astype(jnp.bfloat16)
            copy = to_chip(k, z_out.at[p, k - 1], z_in.at[p, k - 1], z_send.at[p, k - 1], z_recv.at[p, k - 1])
            copy.start()
            copies.append(copy)
        return copies

    def finish(p, z_copies):
        total = sums[p, :, z, core] + mate_in[p, :, z]
        for k, copy in enumerate(z_copies):
            copy.wait_recv()
            total = total + z_in[p, k].astype(jnp.float32)
        here = virt_col[pl.ds(me * rows, rows), 0:1]
        divisor = here + virt_ref[...] - energy_ref[group * per_group + p]
        mine = group * per_group + p
        gathered[mine] = (total / divisor[None]).astype(jnp.bfloat16)
        copies = []
        for k in range(1, groups):
            copy = to_group(
                k, gathered.at[mine], gathered.at[mine], gat_send.at[p, k - 1], gat_recv.at[p, k - 1]
            )
            copy.start()
            copies.append(copy)
        return copies

    mate_copies, z_copies, gat_copies = [], [], []
    for p in range(per_group):
        ladder(p, 0, trips // 2)
        if p > 0:
            z_copies.append(send_z(p - 1, mate_copies[p - 1]))
        ladder(p, trips // 2, trips)
        mate_copies.append(send_mate(p))
        if p > 0:
            gat_copies.append(finish(p - 1, z_copies[p - 1]))
    z_copies.append(send_z(per_group - 1, mate_copies[-1]))
    gat_copies.append(finish(per_group - 1, z_copies[-1]))

    count = jnp.int32(0)
    sources = [jnp.int32(0) for _ in range(capacity)]
    for p in range(pairs_all):
        held = owner_ref[p] == group
        sources = [
            jnp.where(jnp.logical_and(held, count == s), jnp.int32(p), src) for s, src in enumerate(sources)
        ]
        count = count + jnp.where(held, jnp.int32(1), jnp.int32(0))

    for copies in gat_copies:
        for copy in copies:
            copy.wait_recv()
    for s in range(capacity):
        other = partner_ref[sources[s]]
        block = gathered[sources[s]][0].astype(jnp.float32) + gathered[other][1].astype(jnp.float32)
        out_ref[s] = jnp.where(count > s, block, 0.0)

    for copy in list(tile_copies.values()) + fwd_copies + mate_copies:
        copy.wait_send()
    for copies in z_copies + gat_copies:
        for copy in copies:
            copy.wait_send()


def per_device(aux_size, groups, amplitudes, three_index, virt_energy, pair_energy, owner, partner):
    pairs_all, rows, cols = amplitudes.shape
    naux, virt, _ = three_index.shape
    per_group = pairs_all // groups
    capacity = 2 * per_group
    chips = aux_size // 2
    dma = pltpu.SemaphoreType.DMA
    vmem = pl.BlockSpec(memory_space=pltpu.VMEM)
    hbm = pl.BlockSpec(memory_space=pltpu.HBM)
    return pl.pallas_call(
        functools.partial(ladder_kernel, aux_size, groups),
        out_shape=pltpu.VMEM((capacity, rows, virt), jnp.float32),
        in_specs=[hbm] * 6,
        out_specs=vmem,
        scratch_shapes=[
            pltpu.VMEM((1, virt), jnp.float32),
            pltpu.SMEM((pairs_all,), jnp.float32),
            pltpu.SMEM((pairs_all,), jnp.int32),
            pltpu.SMEM((pairs_all,), jnp.int32),
            dma((4,)),
            dma,
            pltpu.VMEM(amplitudes.shape, jnp.bfloat16),
            pltpu.VMEM((groups, rows, per_group * cols), jnp.bfloat16),
            pltpu.VMEM((naux, virt, virt), jnp.bfloat16),
            pltpu.VMEM((aux_size, groups, rows, per_group * cols), jnp.bfloat16),
            pltpu.VMEM((aux_size, per_group, rows, virt), jnp.bfloat16),
            pltpu.VMEM((per_group, 2, chips, 2, rows, virt), jnp.float32),
            pltpu.VMEM((per_group, 2, chips, rows, virt), jnp.float32),
            pltpu.VMEM((per_group, chips - 1, 2, rows, virt), jnp.bfloat16),
            pltpu.VMEM((per_group, chips - 1, 2, rows, virt), jnp.bfloat16),
            pltpu.VMEM((pairs_all, 2, rows, virt), jnp.bfloat16),
            pltpu.VMEM((virt, 128), jnp.float32),
            dma,
            dma((chips, groups)), dma((chips, groups)),
            dma((chips,)), dma((chips,)),
            dma((per_group,)), dma((per_group,)),
            dma((per_group, chips - 1)), dma((per_group, chips - 1)),
            dma((per_group, groups - 1)), dma((per_group, groups - 1)),
        ],
        compiler_params=pltpu.CompilerParams(
            collective_id=0, has_side_effects=True, vmem_limit_bytes=60 * 1024 * 1024
        ),
        cost_estimate=pl.CostEstimate(
            flops=4 * per_group * naux * virt**3, bytes_accessed=2 * naux * virt**2, transcendentals=0
        ),
    )(amplitudes, three_index, virt_energy.reshape(1, virt), pair_energy, owner, partner)


def solution(mesh):
    placed = (P(None, "aux", "pairs"), P("aux", None, None), P(), P(), P(), P())
    return jax.shard_map(
        functools.partial(per_device, mesh.shape["aux"], mesh.shape["pairs"]),
        mesh=mesh, in_specs=placed, out_specs=P("pairs", "aux", None), check_vma=False,
    )
```
